128 devices in a mesh: ctx: 8 (over z_hi, y), head: 16 (over z_lo, x, core).
Axes of the slice: x: 4, y: 4, z: 4 (z_hi: 2, z_lo: 2; z = z_hi * 2 + z_lo), core: 2. Of those that a mesh axis runs over, the one named last changes fastest.
Arguments:
- layer_in: bfloat16 [16, 1024, 2048], P('head', 'ctx'), may hold values from -11 to 11
- cotangent: bfloat16 [16, 1024, 2048], P('head', 'ctx'), may hold values from -6 to 6
- lengths: int32 [16], replicated, may hold values from 256 to 1024, as said below
- weights: float32 [2048, 21504], P(('ctx', 'head')), may hold values from -4 to 4
- weights_first: float32 [2048, 21504], P(('ctx', 'head')), may hold values from -68 to 68
- weights_second: float32 [2048, 21504], P(('ctx', 'head')), may hold values from 0 to 16384, as said below
- gains: float32 [2, 2048], P(None, ('ctx', 'head')), may hold values from 0.5 to 1.5
- gains_first: float32 [2, 2048], P(None, ('ctx', 'head')), may hold values from -68 to 68
- gains_second: float32 [2, 2048], P(None, ('ctx', 'head')), may hold values from 0 to 16384, as said below
Outputs:
- layer_out: bfloat16 [16, 1024, 2048], P('head', 'ctx')
- input_grad: float32 [16, 1024, 2048], P('head', 'ctx')
- weights_new: float32 [2048, 21504], P(('ctx', 'head'))
- weights_first_new: float32 [2048, 21504], P(('ctx', 'head'))
- weights_second_new: float32 [2048, 21504], P(('ctx', 'head'))
- gains_new: float32 [2, 2048], P(None, ('ctx', 'head'))
- gains_first_new: float32 [2, 2048], P(None, ('ctx', 'head'))
- gains_second_new: float32 [2, 2048], P(None, ('ctx', 'head'))
- stream_rms: float32 [5], replicated
The draws below stay inside these ranges and needn't reach their ends.
Inputs may be any that keep to these rules, and one draw needn't show every extreme that they name: `lengths`: one of the 16 slots, chosen by the draw, is full: its length is 1024. `weights_second`: Positive. `gains_second`: Positive.
All inputs are finite; a program needn't handle non-finite values.
Results may differ from the reference program's by a relative error of at most 0.019.
Values may be sent and summed in bfloat16 or wider, within the bound.
No kernel may reach another device: no remote copies, remote signals or barrier semaphores. Data moves between devices by JAX's collectives and lax.ppermute only.
A program may use at most 832 MiB of HBM per device.

```python
import math
import jax
import jax.numpy as jnp
from jax import lax

D = 2048
HEADS = 32
KV = 4
HD = 64
FF = 5632
ADAM_STEP = 5
SLOT = 1024
SEQS = 16
COLS = 21504
N_HEAD = 16


def column_groups():
    column = jnp.arange(COLS, dtype=jnp.int32)
    qkv_end = (HEADS + 2 * KV) * HD
    out_end = qkv_end + HEADS * HD
    gate_end = out_end + 2 * FF
    in_qkv = (column < qkv_end).astype(jnp.float32)
    in_out = ((column >= qkv_end) & (column < out_end)).astype(jnp.float32)
    in_gate = ((column >= out_end) & (column < gate_end)).astype(jnp.float32)
    in_down = (column >= gate_end).astype(jnp.float32)
    return (in_qkv, in_out, in_gate, in_down)


def weight_spread():
    in_qkv, in_out, in_gate, in_down = column_groups()
    return (in_qkv + in_gate) * D ** (-0.5) + in_out * (SLOT / (8.0 * HEADS * HD)) ** 0.5 + in_down * FF ** (-0.5)


def grad_size():
    in_qkv, in_out, in_gate, in_down = column_groups()
    return (0.5 * in_qkv + in_out + 0.3 * in_gate + 0.6 * in_down) * (0.65 * SEQS * SLOT) ** 0.5


def log_between(key, shape, lower, upper):
    return jnp.exp(jax.random.uniform(key, shape, jnp.float32, math.log(lower), math.log(upper)))


def draw_layer_in(key, part):
    key = jax.random.fold_in(key, 11)
    position = jnp.arange(SLOT, dtype=jnp.float32)[None, :, None] / SLOT
    slot_rank = jnp.arange(SEQS, dtype=jnp.float32)[:, None, None] / SEQS
    base_draw = jax.random.truncated_normal(key, -5.0, 5.0, (SEQS, SLOT, D), jnp.float32)
    return (base_draw * (0.5 + 0.8 * position + 0.8 * slot_rank)).astype(jnp.bfloat16)


def draw_lengths(key, part):
    key = jax.random.fold_in(key, 12)
    pick_key, rest_key = jax.random.split(key)
    full_slot = jax.random.randint(pick_key, (), 0, SEQS)
    other_len = jax.random.randint(rest_key, (SEQS,), SLOT // 4, SLOT + 1)
    return jnp.where(jnp.arange(SEQS) == full_slot, SLOT, other_len).astype(jnp.int32)


def draw_weights(key, part):
    key = jax.random.fold_in(key, 13)
    base_draw = jax.random.truncated_normal(key, -4.0, 4.0, (D, COLS), jnp.float32)
    return base_draw * weight_spread()[None, :]


def draw_weights_first(key, part):
    key = jax.random.fold_in(key, 14)
    base_draw = jax.random.truncated_normal(key, -3.0, 3.0, (D, COLS), jnp.float32)
    return base_draw * (0.1 / 0.9) * grad_size()[None, :]


def draw_weights_second(key, part):
    key = jax.random.fold_in(key, 15)
    level_key, entry_key = jax.random.split(key)
    factor = log_between(level_key, (D, COLS), 1.0, 4.0) * log_between(entry_key, (D, COLS), 0.5, 2.0)
    size_sq = grad_size() * grad_size()
    return factor * (0.05 / 0.95) * size_sq[None, :]


def draw_gains_first(key, part):
    key = jax.random.fold_in(key, 16)
    base_draw = jax.random.truncated_normal(key, -3.0, 3.0, (2, D), jnp.float32)
    return base_draw * (0.1 / 0.9) * (0.65 * SEQS * SLOT) ** 0.5


def draw_gains_second(key, part):
    key = jax.random.fold_in(key, 17)
    level_key, entry_key = jax.random.split(key)
    factor = log_between(level_key, (2, D), 1.0, 4.0) * log_between(entry_key, (2, D), 0.5, 2.0)
    return factor * (0.05 / 0.95) * 0.65 * SEQS * SLOT


def block_scale(key, shape, pieces, smallest, high):
    level = 1.0
    for dim, parts in pieces:
        steps = jax.random.uniform(jax.random.fold_in(jax.random.fold_in(key, 6), dim), (parts,), jnp.float32, smallest / len(pieces), high / len(pieces))
        level = level * jnp.repeat(jnp.exp(steps), shape[dim] // parts).reshape((-1,) + (1,) * (len(shape) - 1 - dim))
    return level


def noise(own_key, extent, width, reach, cuts=(), kind=jnp.bfloat16):
    gain = block_scale(own_key, extent, cuts, -0.22, 0.18) if cuts else 1.0
    array = jax.random.normal(own_key, extent, jnp.float32) * width * gain
    return jnp.minimum(jnp.maximum(array, -reach), reach).astype(kind)


def setup_inputs(seed: int = 0) -> dict:
    key_of = jax.random.split(jax.random.key(seed), 10)
    return {
        "layer_in": draw_layer_in(jax.random.fold_in(key_of[9], 71), 0),
        "cotangent": noise(key_of[1], (SEQS, SLOT, D), 1.0, 6.0, ((0, 16), (1, 8))),
        "lengths": draw_lengths(jax.random.fold_in(key_of[9], 71), 0),
        "weights": draw_weights(jax.random.fold_in(key_of[9], 71), 0),
        "weights_first": draw_weights_first(jax.random.fold_in(key_of[9], 71), 0),
        "weights_second": draw_weights_second(jax.random.fold_in(key_of[9], 71), 0),
        "gains": jnp.clip(1.0 + 0.1 * jax.random.normal(key_of[6], (2, D), jnp.float32), 0.5, 1.5),
        "gains_first": draw_gains_first(jax.random.fold_in(key_of[9], 71), 0),
        "gains_second": draw_gains_second(jax.random.fold_in(key_of[9], 71), 0),
    }


@jax.custom_vjp
def low(v):
    return lax.optimization_barrier(v.astype(jnp.bfloat16)).astype(jnp.float32)

@jax.custom_vjp
def low_back(v):
    return v

def low_keep(v):
    return (low(v), None)

def low_pass(kept, grad):
    return (grad,)

def back_keep(v):
    return (v, None)

def back_low(kept, grad):
    return (low(grad),)
low.defvjp(low_keep, low_pass)
low_back.defvjp(back_keep, back_low)
eps_norm = 1e-05
rope_base = 10000.0
beta_first = 0.9
beta_second = 0.95
adam_eps = 1e-08
decay_rate = 0.1
rate_weights = 0.04
rate_gains = 0.3
mask_fill = -1e+30
highest = lax.Precision.HIGHEST

def rope_tables(positions):
    frequency = jnp.power(rope_base, -(jnp.arange(HD // 2, dtype=jnp.float32) * 2.0) / HD)
    angles = positions.astype(jnp.float32)[:, None] * frequency[None, :]
    return (jnp.cos(angles), jnp.sin(angles))

def rotate(values, cosine_table, sine_table):
    half_dim = HD // 2
    lower_half = values[..., :half_dim]
    upper_half = values[..., half_dim:]
    cosine_rows = cosine_table[:, None, :]
    sine_rows = sine_table[:, None, :]
    return jnp.concatenate([lower_half * cosine_rows - upper_half * sine_rows, upper_half * cosine_rows + lower_half * sine_rows], -1)

def normalize(values, gain_row):
    return values * lax.rsqrt(lax.optimization_barrier(jnp.mean(values * values, -1, keepdims=True)) + eps_norm) * gain_row

def attention(query_rot, key_rep, value_rep, lengths):
    qblock = 512 if SLOT % 512 == 0 else SLOT
    block_count = SLOT // qblock
    blocks = query_rot.reshape(SEQS * block_count, qblock, N_HEAD, HEADS // N_HEAD, HD)
    slot_ids = jnp.repeat(jnp.arange(SEQS, dtype=jnp.int32), block_count)
    starts = jnp.tile(jnp.arange(block_count, dtype=jnp.int32) * qblock, SEQS)

    def one_block(inputs):
        query_block, slot_id, first_row = inputs
        key_rows = lax.dynamic_index_in_dim(key_rep, slot_id, 0, keepdims=False)
        value_rows = lax.dynamic_index_in_dim(value_rep, slot_id, 0, keepdims=False)
        length = lax.dynamic_index_in_dim(lengths, slot_id, 0, keepdims=False)
        raw_scores = low_back(jnp.einsum('qghd,kgd->ghqk', query_block, key_rows, precision=highest))
        scores = raw_scores * HD ** (-0.5)
        query_pos = first_row + jnp.arange(qblock, dtype=jnp.int32)
        key_pos = jnp.arange(SLOT, dtype=jnp.int32)
        allowed = (key_pos[None, :] <= query_pos[:, None]) & (key_pos[None, :] < length)
        scores = jnp.where(allowed, scores, mask_fill)
        row_max = lax.optimization_barrier(jnp.max(scores, -1, keepdims=True))
        exp_terms = jnp.exp(scores - row_max)
        softmax_rows = exp_terms / lax.optimization_barrier(jnp.sum(exp_terms, -1, keepdims=True))
        return jnp.einsum('ghqk,kgd->qghd', low(softmax_rows), value_rows, precision=highest)
    attended = lax.map(jax.checkpoint(one_block), (blocks, slot_ids, starts))
    return attended.reshape(SEQS, SLOT, HEADS, HD)

def forward(inputs, weights, gains, lengths):
    wide_params = low(weights)
    gain_rows = low(gains)
    repeats = N_HEAD // KV
    head_cols = HEADS * HD
    kv_cols = KV * HD
    qkv_cols = head_cols + 2 * kv_cols
    out_col = qkv_cols
    gate_col = out_col + head_cols
    down_col = gate_col + 2 * FF
    cosine_table, sine_table = rope_tables(jnp.arange(SLOT, dtype=jnp.int32))
    normed = low(normalize(inputs, gain_rows[0]))
    projected = jnp.dot(normed.reshape(SEQS * SLOT, D), wide_params[:, :qkv_cols], precision=highest).reshape(SEQS, SLOT, qkv_cols)
    query_raw = low_back(projected[..., :head_cols]).reshape(SEQS, SLOT, HEADS, HD)
    key_raw = low_back(projected[..., head_cols:head_cols + kv_cols]).reshape(SEQS, SLOT, KV, HD)
    value_raw = low_back(projected[..., head_cols + kv_cols:]).reshape(SEQS, SLOT, KV, HD)
    query_rot = low_back(low(rotate(query_raw, cosine_table, sine_table)))
    key_rep = low_back(jnp.repeat(low(rotate(key_raw, cosine_table, sine_table)), repeats, axis=2))
    value_rep = low_back(jnp.repeat(low(value_raw), repeats, axis=2))
    attended = attention(query_rot.reshape(SEQS, SLOT, N_HEAD, HEADS // N_HEAD, HD), key_rep, value_rep, lengths)
    attended = low_back(low(attended)).reshape(SEQS * SLOT, head_cols)
    branch = low_back(jnp.dot(attended, wide_params[:, out_col:gate_col].T, precision=highest)).reshape(SEQS, SLOT, D)
    middle = inputs + branch
    normed_mid = low(normalize(middle, gain_rows[1]))
    gate_up = jnp.dot(normed_mid.reshape(SEQS * SLOT, D), wide_params[:, gate_col:down_col], precision=highest)
    gate_pre = low_back(gate_up[:, :FF])
    up_pre = low_back(gate_up[:, FF:])
    hidden = low(jax.nn.silu(gate_pre) * up_pre)
    mlp_out = low_back(jnp.dot(hidden, wide_params[:, down_col:].T, precision=highest)).reshape(SEQS, SLOT, D)
    result = middle + mlp_out
    return (result, (branch, middle, mlp_out))

def adam(param_now, first_old, second_old, grad_now, step_rate, decay_now):
    first_new = beta_first * first_old + (1.0 - beta_first) * grad_now
    second_new = beta_second * second_old + (1.0 - beta_second) * grad_now * grad_now
    corr_first = 1.0 - beta_first ** ADAM_STEP
    corr_second = 1.0 - beta_second ** ADAM_STEP
    update = first_new / corr_first / (jnp.sqrt(second_new / corr_second) + adam_eps) + decay_now * param_now
    return (param_now - step_rate * update, first_new, second_new)

def reference(layer_in, cotangent, lengths, weights, weights_first, weights_second, gains, gains_first, gains_second):
    inputs = layer_in.astype(jnp.float32)

    def wrapped(inputs, weights, gains):
        return forward(inputs, weights, gains, lengths)
    result, pullback, extras = jax.vjp(wrapped, inputs, weights, gains, has_aux=True)
    branch, middle, mlp_out = extras
    valid_rows = (jnp.arange(SLOT, dtype=jnp.int32)[None, :] < lengths[:, None]).astype(jnp.float32)
    back_rows = cotangent.astype(jnp.float32) * valid_rows[..., None]
    input_grad, weight_grad, gain_grad = pullback(back_rows)
    valid_mask = valid_rows[..., None]
    streams = jnp.stack([jnp.sum(inputs * inputs * valid_mask), jnp.sum(middle * middle * valid_mask), jnp.sum(result * result * valid_mask), jnp.sum(branch * branch * valid_mask), jnp.sum(mlp_out * mlp_out * valid_mask)])
    valid_count = jnp.sum(valid_rows) * D
    stream_rms = jnp.sqrt(streams / valid_count)
    weights_new, weights_first_new, weights_second_new = adam(weights, weights_first, weights_second, weight_grad, rate_weights, decay_rate)
    gains_new, gains_first_new, gains_second_new = adam(gains, gains_first, gains_second, gain_grad, rate_gains, 0.0)
    return (result.astype(jnp.bfloat16), input_grad, weights_new, weights_first_new, weights_second_new, gains_new, gains_first_new, gains_second_new, stream_rms)
```

```python
import functools

import jax
import jax.numpy as jnp
from jax import lax
from jax.experimental import pallas as pl
from jax.experimental.pallas import tpu as pltpu
from jax.sharding import Mesh, PartitionSpec as P

D = 2048
HEADS = 32
KV = 4
HD = 64
FF = 5632
ADAM_STEP = 5

eps_norm = 1e-05
rope_base = 10000.0
beta_first = 0.9
beta_second = 0.95
adam_eps = 1e-08
decay_rate = 0.1
rate_weights = 0.04
rate_gains = 0.3
mask_fill = -1e30

PLANE = ("zh", "zl", "x")
EVERY = ("zh", "y", "zl", "x", "core")
T = 8
ROWS = 128
QB = 256
GROUP_HEADS = HEADS // T
Q_LOC = GROUP_HEADS * HD
N_QKV = Q_LOC + 2 * HD
FF_LOC = FF // T
FULL_TILES = FF_LOC // 128
GU = 2 * FF_LOC
DOWN = 768
N_ATTN = N_QKV + Q_LOC
ATTN_COLS = 2 * HEADS * HD + 2 * KV * HD
NN = (((1,), (0,)), ((), ()))
NT = (((1,), (1,)), ((), ()))
TN = (((0,), (0,)), ((), ()))
f32 = jnp.float32
bf16 = jnp.bfloat16


def mul(a, b, dims=NN):
    return lax.dot_general(a, b, dims, preferred_element_type=f32)


def rope_tables(positions):
    frequency = jnp.power(rope_base, -(jnp.arange(HD // 2, dtype=f32) * 2.0) / HD)
    angles = positions.astype(f32)[:, None] * frequency[None, :]
    cosine, sine = jnp.cos(angles), jnp.sin(angles)
    return jnp.concatenate([cosine, cosine, -sine, sine], 1)


def rms_factor(values):
    return lax.rsqrt(jnp.mean(values * values, -1, keepdims=True) + eps_norm)


def adam(param_now, first_old, second_old, grad_now, step_rate, decay_now):
    first_new = beta_first * first_old + (1.0 - beta_first) * grad_now
    second_new = beta_second * second_old + (1.0 - beta_second) * grad_now * grad_now
    corr_first = 1.0 - beta_first**ADAM_STEP
    corr_second = 1.0 - beta_second**ADAM_STEP
    update = (
        first_new / corr_first / (jnp.sqrt(second_new / corr_second) + adam_eps)
        + decay_now * param_now
    )
    return (param_now - step_rate * update, first_new, second_new)


def trade(values, axis, step):
    return lax.ppermute(values, axis, [(i, i ^ step) for i in range(4)])


def tie(*values):
    return lax.optimization_barrier(values)


def during(send, operand, work, *args):
    return tie(send(operand), work(*args))


def swap_core(values):
    return lax.ppermute(values, "core", [(0, 1), (1, 0)])


def send_near(own, axis):
    return trade(own, axis, 1), trade(own, axis, 3)


def send_far(halves, axis):
    return trade(halves[0], axis, 3), trade(halves[1], axis, 1)


def sum_far(halves, axis):
    return trade(halves[0], axis, 1), trade(halves[1], axis, 3)


def sum_near(joined, axis):
    return trade(joined[0], axis, 1), trade(joined[1], axis, 3)


def other_half(values):
    return lax.ppermute(values, ("zh", "core"), [(1, 2), (2, 1)])


def swap_halves(values):
    other = other_half(values)
    return jnp.where(lax.axis_index("zh") == lax.axis_index("core"), values, other)


def pick(values, index, axis=0):
    return lax.dynamic_index_in_dim(values, index, axis, keepdims=False)


def place(pieces, index):
    odd, high = (index & 1) == 1, (index & 2) == 2
    return jnp.stack(
        [
            jnp.where(
                high,
                jnp.where(odd, pieces[k ^ 3], pieces[k ^ 2]),
                jnp.where(odd, pieces[k ^ 1], pieces[k]),
            )
            for k in range(4)
        ]
    )


def exchange_cores(parts):
    core = lax.axis_index("core")
    parts = parts.reshape(4, 2, 16, -1)
    kept = pick(parts, core, 1)
    came = swap_core(pick(parts, 1 - core, 1))
    return jnp.concatenate(
        [jnp.where(core == 0, kept, came), jnp.where(core == 0, came, kept)], 1
    )


def exchange_y(both):
    y = lax.axis_index("y")
    return [pick(both, y)] + [trade(pick(both, y ^ k), "y", k) for k in (1, 2, 3)]


def arrange(pieces):
    return place(pieces, lax.axis_index("y")).reshape(ROWS, -1)


def exchange(parts):
    return arrange(exchange_y(exchange_cores(parts)))


def order_matrix():
    source = lax.broadcasted_iota(jnp.int32, (1024, 1024), 0)
    target = lax.broadcasted_iota(jnp.int32, (1024, 1024), 1)
    want = (target % 128) // 32 * 256 + target // 128 * 32 + target % 32
    return (source == want).astype(bf16)


def call(body, name, out_shape, flops, limit=24, scratch=(), **kw):
    return pl.pallas_call(
        body,
        out_shape=out_shape,
        scratch_shapes=list(scratch),
        compiler_params=pltpu.CompilerParams(vmem_limit_bytes=limit * 2**20),
        cost_estimate=pl.CostEstimate(flops=1, bytes_accessed=1, transcendentals=0),
        name=name,
        **kw,
    )


def whole(n):
    return [pl.BlockSpec(memory_space=pltpu.VMEM)] * n


def anywhere(n):
    return [pl.BlockSpec(memory_space=pl.ANY)] * n


def hbm(n):
    return [pl.BlockSpec(memory_space=pltpu.HBM)] * n


def fetch(blocks, target, sems):
    copies = [
        pltpu.make_async_copy(block, target.at[pl.ds(i * ROWS, ROWS), :], sems.at[i])
        for i, block in enumerate(blocks)
    ]
    for copy in copies:
        copy.start()
    return copies


def turn_tables(table):
    low = lax.broadcasted_iota(jnp.int32, table.shape, 1) < HD
    other = pltpu.roll(table, HD, 1)
    return jnp.where(low, table, other), jnp.where(low, other, table)


def halves_swapped(values):
    width = values.shape[1]
    lane = lax.broadcasted_iota(jnp.int32, values.shape, 1)
    return jnp.where(
        lane % HD < HD // 2,
        pltpu.roll(values, width - HD // 2, 1),
        pltpu.roll(values, HD // 2, 1),
    )


def heads_down(values):
    return jnp.concatenate([values[:, h * HD : (h + 1) * HD] for h in range(GROUP_HEADS)], 0)


def heads_across(columns):
    pairs = []
    for h in range(0, GROUP_HEADS, 2):
        pair = jnp.concatenate(
            [columns[:, h * QB : (h + 1) * QB], columns[:, (h + 1) * QB : (h + 2) * QB]], 0
        )
        pairs.append(pair.T)
    return jnp.concatenate(pairs, 1)


def causal(scores, block, length):
    key_pos = block * QB + lax.broadcasted_iota(jnp.int32, scores.shape, 0)
    query_pos = block * QB + lax.broadcasted_iota(jnp.int32, scores.shape, 1) % QB
    return jnp.where((key_pos <= query_pos) & (key_pos < length), scores, mask_fill)


def in_length(scores, block, length):
    key_pos = block * QB + lax.broadcasted_iota(jnp.int32, (QB, 1), 0)
    return scores + jnp.where(key_pos < length, 0.0, mask_fill)


def project(info, *refs):
    wide_ref, table_ref = refs[8:10]
    q_ref, k_ref, v_ref, kt_ref, vt_ref, w_ref, out_ref, proj, rows, sems, w_sems = refs[10:]
    w_copies = [
        pltpu.make_async_copy(wide_ref.at[:, pl.ds(at, width)], target, w_sems.at[i])
        for i, (at, width, target) in enumerate(((0, N_QKV, w_ref), (N_QKV, Q_LOC, out_ref)))
    ]
    for copy in w_copies:
        copy.start()
    copies = fetch(refs[:8], rows, sems)
    w_copies[0].wait()
    for k in range(4):
        copies[2 * k].wait()
        copies[2 * k + 1].wait()
        part = mul(rows[pl.ds(2 * k * ROWS, 2 * ROWS), :], w_ref[...])
        for i in range(2):
            at = pl.multiple_of(info[2 * k + i], ROWS)
            proj[pl.ds(at, ROWS), :] = part[i * ROWS : (i + 1) * ROWS]

    def turn(b, carry):
        at = pl.ds(pl.multiple_of(b * QB, QB), QB)
        part = proj[at, :]
        cosine, sine = turn_tables(table_ref[at, :])
        query = part[:, :Q_LOC]
        query = query * jnp.concatenate([cosine] * 2, 1) + halves_swapped(
            query
        ) * jnp.concatenate([sine] * 2, 1)
        q_ref[b] = heads_down(query * HD**-0.5).astype(bf16)
        pair = part[:, Q_LOC:]
        key = pair * cosine + halves_swapped(pair) * sine
        k_ref[b] = key[:, :HD].astype(bf16)
        kt_ref[b] = key.T[:HD].astype(bf16)
        v_ref[b] = pair[:, HD:].astype(bf16)
        vt_ref[b] = pair.T[HD:].astype(bf16)
        return carry

    lax.fori_loop(0, T * ROWS // QB, turn, 0)
    w_copies[1].wait()


def attend(info, q_ref, k_ref, vt_ref, att_ref, log_ref, out):
    length = info[8]

    def one(b, carry):
        query = q_ref[b]
        scores = causal(mul(k_ref[b], query, NT), b, length)
        top = jnp.max(scores, 0, keepdims=True)
        terms = jnp.exp(scores - top)
        bottom = jnp.sum(terms, 0, keepdims=True)
        acc = mul(vt_ref[b], terms.astype(bf16))

        def earlier(k, state):
            top, bottom, acc = state
            scores = in_length(mul(k_ref[k], query, NT), k, length)
            new_top = jnp.maximum(top, jnp.max(scores, 0, keepdims=True))
            terms = jnp.exp(scores - new_top)
            fade = jnp.exp(top - new_top)
            bottom = bottom * fade + jnp.sum(terms, 0, keepdims=True)
            return new_top, bottom, acc * fade + mul(vt_ref[k], terms.astype(bf16))

        top, bottom, acc = lax.fori_loop(0, b, earlier, (top, bottom, acc))
        log_ref[b] = top + jnp.log(bottom)
        at = pl.ds(pl.multiple_of(b * QB, QB), QB)
        out[at, :] = heads_across(acc / bottom).astype(bf16)
        return carry

    lax.fori_loop(0, T * ROWS // QB, one, 0)
    for k in range(8):
        at = pl.multiple_of(info[k], ROWS)
        att_ref[pl.ds(k * ROWS, ROWS), :] = out[pl.ds(at, ROWS), :]


def row_terms(steps, rows_ref, w_ref, *outs):
    for i, k in enumerate(steps):
        part = mul(rows_ref[pl.ds(2 * k * ROWS, 2 * ROWS), :], w_ref[...], NT).astype(bf16)
        outs[2 * i][...] = part[:ROWS]
        outs[2 * i + 1][...] = part[ROWS:]


def last_grads(steps, info, rows_ref, w_ref, *refs):
    blocks, held, refs = refs[:8], refs[8], refs[9:]
    rows, grads, sems, held_sems = refs[-4:]
    far_a, far_b, one, three, own = refs[-9:-4]
    copies = fetch(blocks, rows, sems)
    targets = [
        (2, 0, 2, far_a),
        (2, 2, 2, far_b),
        (1, 0, 4, one),
        (3, 0, 4, three),
        (0, 0, 4, own),
    ]
    held_copies = []
    for k, first, count, target in targets:
        for i in range(count):
            at = pl.multiple_of((first + i) * 4 * ROWS + info[13 + k], ROWS)
            held_copies.append(
                pltpu.make_async_copy(
                    held.at[pl.ds(at, ROWS), :],
                    target.at[pl.ds(i * ROWS, ROWS), pl.ds(N_QKV, Q_LOC)],
                    held_sems.at[len(held_copies)],
                )
            )
    for copy in held_copies:
        copy.start()
    row_terms(steps, rows_ref, w_ref, *refs[:-9])
    for copy in copies:
        copy.wait()

    def outer(i, carry):
        at = pl.ds(pl.multiple_of(i * 256, 256), 256)
        grads[at, :] = mul(rows[:, at], rows_ref[...], TN).astype(bf16)
        return carry

    lax.fori_loop(0, D // 256, outer, 0)
    for k, first, count, target in targets:
        for i in range(count):
            at = pl.multiple_of((first + i) * 4 * ROWS + info[13 + k], ROWS)
            target[i * ROWS : (i + 1) * ROWS, :N_QKV] = grads[pl.ds(at, ROWS), :]
    for copy in held_copies:
        copy.wait()


def reorder(values, matrix, dims):
    return jnp.concatenate(
        [mul(values[:, :1024], matrix, dims), mul(values[:, 1024:], matrix, dims)], 1
    )


def valid_rows(info, shape):
    return info[0] + lax.broadcasted_iota(jnp.int32, shape, 0) < info[8]


def take_inputs(info, here_ref, other_ref, matrix_ref, inputs_ref, normed_ref):
    rows = jnp.where(info[17] == 1, here_ref[...].astype(f32), other_ref[0].astype(f32))
    rows = reorder(rows.astype(bf16), matrix_ref[...], NN)
    inputs_ref[...] = rows.astype(bf16)
    normed_ref[...] = (rows * rms_factor(rows)).astype(bf16)


def take_cotangent(info, here_ref, other_ref, matrix_ref, out_ref):
    rows = jnp.where(info[17] == 1, here_ref[...].astype(f32), other_ref[1].astype(f32))
    rows = reorder(rows.astype(bf16), matrix_ref[...], NN)
    out_ref[...] = jnp.where(valid_rows(info, (ROWS, 1)), rows, 0.0).astype(bf16)


def cut(one, three, first, second):
    half = one.shape[0] // 2
    first[...] = one[:half]
    second[...] = three[half:]


def sum_of(*refs):
    total = refs[0][...].astype(f32)
    for ref in refs[1:]:
        total = total + ref[...].astype(f32)
    return total


def far_sum(kept, came, first, second):
    half = kept.shape[0] // 2
    total = sum_of(kept, came).astype(bf16)
    first[...] = total[:half]
    second[...] = total[half:]


def near_join(*refs):
    count = (len(refs) - 4) // 2
    came_one, came_three, one_ref, three_ref = refs[-4:]
    half = came_one.shape[0]
    one, three = sum_of(*refs[:count]), sum_of(*refs[count : 2 * count])
    one_ref[:half] = one[:half].astype(bf16)
    one_ref[half:] = (one[half:] + came_three[...].astype(f32)).astype(bf16)
    three_ref[:half] = (three[:half] + came_one[...].astype(f32)).astype(bf16)
    three_ref[half:] = three[half:].astype(bf16)


def take_middle(*refs):
    inputs_ref, middle_ref, normed_ref = refs[4:]
    middle = inputs_ref[...].astype(f32) + sum_of(*refs[:4])
    middle_ref[...] = middle
    normed_ref[...] = (middle * rms_factor(middle)).astype(bf16)


def norm_back(term, values):
    scale = rms_factor(values)
    inner = jnp.mean(term * values, -1, keepdims=True)
    return scale * (term - values * (scale * scale * inner))


def middle_grads(*refs):
    middle_ref, back_ref, grad_ref, low_ref = refs[4:]
    grad = back_ref[...].astype(f32) + norm_back(sum_of(*refs[:4]), middle_ref[...])
    grad_ref[...] = grad
    low_ref[...] = grad.astype(bf16)


def give_output(info, *refs):
    middle_ref, inputs_ref, matrix_ref, out_ref, streams_ref = refs[4:]
    mlp_out = sum_of(*refs[:4])
    middle, inputs = middle_ref[...], inputs_ref[...].astype(f32)
    result = middle + mlp_out
    out_ref[...] = reorder(result.astype(bf16), matrix_ref[...], NT).astype(bf16)
    valid = valid_rows(info, (ROWS, 1))
    streams_ref[...] = jnp.zeros(streams_ref.shape, f32)
    for i, stream in enumerate((inputs, middle, result, middle - inputs, mlp_out)):
        squares = jnp.sum(jnp.where(valid, stream * stream, 0.0), 0, keepdims=True)
        lanes = squares[:, :128]
        for j in range(1, D // 128):
            lanes = lanes + squares[:, j * 128 : (j + 1) * 128]
        streams_ref[i : i + 1, :] = lanes


def give_input_grad(*refs):
    inputs_ref, middle_grad_ref, matrix_ref, out_ref = refs[4:]
    grad = middle_grad_ref[...] + norm_back(sum_of(*refs[:4]), inputs_ref[...].astype(f32))
    out_ref[...] = reorder(grad.astype(bf16), matrix_ref[...], NT).astype(bf16)


def split_streams(streams):
    high = streams.astype(bf16).astype(f32)
    rest = streams - high
    middle = rest.astype(bf16).astype(f32)
    low = rest - middle
    return jnp.concatenate([high, middle], 0), jnp.concatenate([low, jnp.zeros_like(low)], 0)


def join_streams(first, second):
    return first[:8] + (first[8:] + second[:8])


def sum_lines(info, own, one, three, streams_ref, *outs):
    first, second = split_streams(streams_ref[...])
    rows = jnp.concatenate([first, second, jnp.zeros((ROWS - 32, 128), f32)], 0).astype(bf16)
    for k in range(4):
        at = pl.ds(pl.multiple_of(lax.div(info[9 + k], 4), ROWS), ROWS)
        part = own[at, :].astype(f32) + one[at, :].astype(f32) + three[at, :].astype(f32)
        outs[k][:, : part.shape[1]] = part.astype(outs[k].dtype)
        if k:
            outs[k][:, part.shape[1] :] = rows


def prepare(gains_ref, w_ref, attn_ref, mlp_ref):
    first_gain, second_gain = gains_ref[:, 0:1], gains_ref[:, 1:2]

    def low(at, width):
        return w_ref[:, at : at + width].astype(bf16)

    def scaled(at, width, gain):
        return (low(at, width).astype(f32) * gain).astype(bf16)

    key, value = HEADS * HD, (HEADS + KV) * HD
    out = (HEADS + 2 * KV) * HD
    gate = out + HEADS * HD
    for t in range(T):
        attn_ref[t, :, :Q_LOC] = scaled(t * Q_LOC, Q_LOC, first_gain)
        attn_ref[t, :, N_QKV:N_ATTN] = low(out + t * Q_LOC, Q_LOC)
    for h in range(KV):
        tile = h // 2 * 2 * HD
        lanes = slice(h % 2 * HD, h % 2 * HD + HD)
        pair = jnp.concatenate(
            [
                scaled(key + tile, 2 * HD, first_gain).astype(f32)[:, lanes],
                scaled(value + tile, 2 * HD, first_gain).astype(f32)[:, lanes],
            ],
            1,
        ).astype(bf16)
        for t in (2 * h, 2 * h + 1):
            attn_ref[t, :, Q_LOC:N_QKV] = pair
    for i in range(3):
        for t in range(T):
            start = gate + i * FF + t * FF_LOC
            for j in range(FULL_TILES + 1):
                at = start + j * 128
                if t % 2 == 0:
                    tile = w_ref[:, at : at + 128]
                elif j < FULL_TILES:
                    tile = jnp.concatenate(
                        [w_ref[:, at - 64 : at + 64][:, 64:], w_ref[:, at + 64 : at + 192][:, :64]], 1
                    )
                else:
                    tile = pltpu.roll(w_ref[:, at - 64 : at + 64], 64, 1)
                tile = tile.astype(bf16).astype(f32)
                if i < 2:
                    tile = tile * second_gain
                if j < FULL_TILES:
                    target = mlp_ref if i < 2 else attn_ref
                    to = j * 256 + i * 128 if i < 2 else N_ATTN + j * 128
                    target[t, :, to : to + 128] = tile.astype(bf16)
                elif i == 0:
                    gate_tile = tile
                elif i == 1:
                    last_up = tile
                else:
                    lane = lax.broadcasted_iota(jnp.int32, tile.shape, 1)
                    attn_ref[t, :, N_ATTN + FULL_TILES * 128 :] = jnp.where(
                        lane < 64, tile, 0.0
                    ).astype(bf16)
            if i == 0:
                tails = [] if t == 0 else tails
                tails.append(gate_tile)
            elif i == 1:
                lane = lax.broadcasted_iota(jnp.int32, last_up.shape, 1)
                mlp_ref[t, :, FULL_TILES * 256 : GU] = jnp.where(
                    lane < 64, tails[t], pltpu.roll(last_up, 64, 1)
                ).astype(bf16)


def plane_parts(own, one, two, three, streams_ref, out_ref):
    width = N_QKV + Q_LOC
    total = own[...]
    streams = [streams_ref[...]]
    for ref in (one, two, three):
        total = total + ref[:, :width].astype(f32)
        rows = ref[:32, width:].astype(f32)
        streams.append(join_streams(rows[:16], rows[16:]))
    total = total.astype(bf16)
    first, second = split_streams((streams[0] + streams[1]) + (streams[2] + streams[3]))
    for t in range(T):
        out_ref[t, :, :width] = total[t * 16 : t * 16 + 16]
        out_ref[t, :, width : width + 128] = first.astype(bf16)
        out_ref[t, :, width + 128 :] = second.astype(bf16)


def adam_columns(base, at, grad, refs):
    w_ref, first_ref, second_ref, w_out, first_out, second_out = refs
    source = slice(base + at, base + at + grad.shape[1])
    columns = slice(at, at + grad.shape[1])
    results = adam(
        w_ref[:, source],
        first_ref[:, source],
        second_ref[:, source],
        grad,
        rate_weights,
        decay_rate,
    )
    for ref, value in zip((w_out, first_out, second_out), results):
        ref[:, columns] = value
    return at + grad.shape[1]


def weighed(w_ref, at, grad):
    weight = w_ref[:, at : at + grad.shape[1]].astype(bf16).astype(f32)
    return jnp.sum(weight * grad, 1, keepdims=True)


def send_columns(base, buffers, outs, sems):
    copies = [
        pltpu.make_async_copy(buffer, out.at[:, pl.ds(base, buffer.shape[1])], sems.at[i])
        for i, (buffer, out) in enumerate(zip(buffers, outs))
    ]
    for copy in copies:
        copy.start()
    for copy in copies:
        copy.wait()


def update_mlp(gains_ref, mlp_ref, *refs):
    outs, sums_ref, buffers, sems = refs[3:6], refs[6], refs[7:10], refs[10]
    refs = refs[:3] + buffers
    second_gain = gains_ref[:, 1:2]

    def mlp(t, first, last):
        return mlp_ref[t, :, first:last].astype(f32)

    def columns(tiles, tail):
        for t in range(0, T, 2):
            low = [mlp(t, *tiles(j)) for j in range(FULL_TILES)] + [mlp(t, *tail)]
            high = [mlp(t + 1, *tiles(j)) for j in range(FULL_TILES)] + [mlp(t + 1, *tail)]
            yield from low[:FULL_TILES]
            before = low[FULL_TILES]
            for tile in high[:FULL_TILES]:
                yield jnp.concatenate([before, tile[:, :64]], 1)
                before = tile[:, 64:]
            yield jnp.concatenate([before, high[FULL_TILES]], 1)

    at = 0
    total = jnp.zeros((16, 1), f32)
    last = FULL_TILES * 256
    for i in range(2):
        for grad in columns(
            lambda j: (j * 256 + i * 128, j * 256 + i * 128 + 128),
            (last + i * 64, last + i * 64 + 64),
        ):
            total = total + weighed(refs[0], ATTN_COLS + at, grad)
            at = adam_columns(ATTN_COLS, at, grad * second_gain, refs)
    sums_ref[...] = total + jnp.zeros(sums_ref.shape, f32)
    for grad in columns(
        lambda j: (GU + j * 128, GU + j * 128 + 128), (GU + FF_LOC - 64, GU + FF_LOC)
    ):
        at = adam_columns(ATTN_COLS, at, grad, refs)
    send_columns(ATTN_COLS, buffers, outs, sems)


def update_attention(gains_ref, attn_ref, *refs):
    outs, sums_ref, streams_ref, refs = refs[6:9], refs[9], refs[10], refs[:3] + refs[11:]
    buffers, sems = refs[3:6], refs[9]
    copies = [
        pltpu.make_async_copy(ref.at[:, pl.ds(0, ATTN_COLS)], buffer, sems.at[i])
        for i, (ref, buffer) in enumerate(zip(refs[:3], refs[6:9]))
    ]
    for copy in copies:
        copy.start()
    width = N_QKV + Q_LOC
    streams = jnp.zeros(streams_ref.shape, f32)
    for t in range(T):
        streams = streams + join_streams(
            attn_ref[t, :, width : width + 128].astype(f32), attn_ref[t, :, width + 128 :].astype(f32)
        )
    streams_ref[...] = streams
    for copy in copies:
        copy.wait()
    refs = refs[6:9] + buffers
    first_gain = gains_ref[:, 0:1]

    def attn(t, first, last):
        return attn_ref[t, :, first:last].astype(f32)

    at = 0
    total = jnp.zeros((16, 1), f32)
    for t in range(T):
        grad = attn(t, 0, Q_LOC)
        total = total + weighed(refs[0], at, grad)
        at = adam_columns(0, at, grad * first_gain, refs)
    for first in (Q_LOC, Q_LOC + HD):
        heads = [
            attn(t, first, first + HD) + attn(t + 1, first, first + HD) for t in range(0, T, 2)
        ]
        for h in range(0, KV, 2):
            grad = jnp.concatenate(heads[h : h + 2], 1)
            total = total + weighed(refs[0], at, grad)
            at = adam_columns(0, at, grad * first_gain, refs)
    for t in range(T):
        at = adam_columns(0, at, attn(t, N_QKV, N_QKV + Q_LOC), refs)
    sums_ref[...] = total + jnp.zeros(sums_ref.shape, f32)
    send_columns(0, buffers, outs, sems)


def head_grads(mine, theirs, w_ref, out_ref, rows, sems):
    for copy in fetch((mine, theirs), rows, sems):
        copy.wait()
    out_ref[...] = mul(rows[...], w_ref[...]).astype(bf16)


def attention_backward(first, count, info, *refs):
    grads, att_ref, refs = refs[:4], refs[4], refs[5:]
    table_ref, q_ref, k_ref, v_ref, kt_ref, log_ref = refs[:6]
    last = first + count == T * ROWS // QB
    if first:
        dk_in, dv_in, proj_in, refs = refs[6], refs[7], refs[8], refs[9:]
    else:
        refs = refs[6:]
    if last:
        blocks, refs = refs[:8], refs[8:]
        proj_ref, out_ref, grad, prod, dk, dv, proj, rows, sems = refs
        copies = fetch(blocks, rows, sems)
    else:
        dk, dv, proj, grad, prod = refs
    length = info[8]
    for k in range(4):
        part = grads[k][...].astype(f32)
        both = part * att_ref[pl.ds(2 * k * ROWS, 2 * ROWS), :].astype(f32)
        for i in range(2):
            at = pl.multiple_of(info[2 * k + i], ROWS)
            grad[pl.ds(at, ROWS), :] = part[i * ROWS : (i + 1) * ROWS]
            prod[pl.ds(at, ROWS), :] = both[i * ROWS : (i + 1) * ROWS]
    if first:
        dk[...] = dk_in[...]
        dv[...] = dv_in[...]
        proj[...] = proj_in[...]
    else:
        dk[...] = jnp.zeros_like(dk)
        dv[...] = jnp.zeros_like(dv)
        proj[...] = jnp.zeros_like(proj)

    def block(b, carry):
        at = pl.ds(pl.multiple_of(b * QB, QB), QB)
        query = q_ref[b]
        out_grad = heads_down(grad[at, :]).astype(bf16)
        by_lane = prod[at, :].T
        delta = jnp.concatenate(
            [
                jnp.sum(by_lane[h * HD : (h + 1) * HD], 0, keepdims=True)
                for h in range(GROUP_HEADS)
            ],
            1,
        )
        logs = log_ref[b]

        def one(k, dq, mask):
            scores = mask(mul(k_ref[k], query, NT), k, length)
            probs = jnp.exp(scores - logs)
            share_grad = mul(v_ref[k], out_grad, NT)
            score_grad = (probs * (share_grad - delta)).astype(bf16)
            dv[k] += mul(probs.astype(bf16), out_grad)
            dk[k] += mul(score_grad, query)
            return dq + mul(kt_ref[k], score_grad)

        dq = one(b, jnp.zeros((HD, GROUP_HEADS * QB), f32), causal)
        dq = lax.fori_loop(0, b, lambda k, dq: one(k, dq, in_length), dq)
        query_grad = heads_across(dq * HD**-0.5).astype(bf16).astype(f32)
        cosine, sine = turn_tables(table_ref[at, :])
        proj[at, :] = query_grad * jnp.concatenate([cosine] * 2, 1) - halves_swapped(
            query_grad
        ) * jnp.concatenate([sine] * 2, 1)
        return carry

    lax.fori_loop(first, first + count, block, 0)
    if not last:
        return
    for k in range(8):
        at = pl.ds(pl.multiple_of(info[k], ROWS), ROWS)
        to = pl.ds(k * ROWS, ROWS)
        proj_ref[to, :Q_LOC] = proj[at, :].astype(bf16)
        b = lax.div(info[k], QB)
        inner = pl.ds(pl.multiple_of(lax.rem(info[k], QB), ROWS), ROWS)
        pair = jnp.concatenate([dk[b, inner, :], dv[b, inner, :]], 1)
        cosine, sine = turn_tables(table_ref[at, :])
        turned = pair * cosine - halves_swapped(pair) * sine
        lane = lax.broadcasted_iota(jnp.int32, pair.shape, 1)
        proj_ref[to, Q_LOC:] = jnp.where(lane < HD, turned, pair).astype(bf16)
    for copy in copies:
        copy.wait()

    def outer(i, carry):
        at = pl.ds(pl.multiple_of(i * 256, 256), 256)
        out_ref[at, :] = mul(rows[:, at], att_ref[...], TN).astype(bf16)
        return carry

    lax.fori_loop(0, D // 256, outer, 0)


def mlp_pair(*refs):
    w_ref, wide_ref = refs[4:6]
    hidden_ref, grad_ref, kept, sent, out_kept, out_sent = refs[6:12]
    hidden_grad, grads_buf, rows_buf, grad_sems, row_sems = refs[12:]
    grad_copies = fetch(refs[2:4], grads_buf, grad_sems)
    row_copies = fetch(refs[:2], rows_buf, row_sems)
    for copy in grad_copies:
        copy.wait()
    hidden_grad[...] = mul(grads_buf[...], wide_ref[:, N_ATTN:])
    for copy in row_copies:
        copy.wait()
    rows = rows_buf[...]

    def both_grads(gate, up, back):
        gate_on = jax.nn.sigmoid(gate)
        silu = gate * gate_on
        return silu * up, back * up * gate_on * (1.0 + gate * (1.0 - gate_on)), back * silu

    for j in range(FULL_TILES):
        gate_up = mul(rows, w_ref[:, j * 256 : (j + 1) * 256])
        tile = pl.ds(j * 128, 128)
        hidden, gate_grad, up_grad = both_grads(
            gate_up[:, :128], gate_up[:, 128:], hidden_grad[:, tile]
        )
        hidden_ref[:, tile] = hidden.astype(bf16)
        grad_ref[:, pl.ds(j * 256, 128)] = gate_grad.astype(bf16)
        grad_ref[:, pl.ds(j * 256 + 128, 128)] = up_grad.astype(bf16)
    gate_up = mul(rows, w_ref[:, FULL_TILES * 256 : GU])
    tile = pl.ds(FULL_TILES * 128, 128)
    low = lax.broadcasted_iota(jnp.int32, gate_up.shape, 1) < 64
    turned = pltpu.roll(gate_up, 64, 1)
    back = hidden_grad[:, tile]
    back = jnp.where(low, back, pltpu.roll(back, 64, 1))
    hidden, gate_grad, up_grad = both_grads(
        jnp.where(low, gate_up, turned), jnp.where(low, turned, gate_up), back
    )
    hidden_ref[:, tile] = jnp.where(low, hidden, 0.0).astype(bf16)
    grad_ref[:, pl.ds(FULL_TILES * 256, 128)] = jnp.where(low, gate_grad, up_grad).astype(bf16)

    def back_block(n, carry):
        at = pl.ds(pl.multiple_of(n * 256, 256), 256)
        part = mul(grad_ref[...], w_ref[at, :], NT).astype(bf16)
        kept[:, at] = part[:ROWS]
        sent[:, at] = part[ROWS:]
        part = mul(hidden_ref[...], wide_ref[at, N_ATTN:], NT).astype(bf16)
        out_kept[:, at] = part[:ROWS]
        out_sent[:, at] = part[ROWS:]
        return carry

    lax.fori_loop(0, D // 256, back_block, 0)


def outer_sums(groups, copied, *refs):
    out_ref = refs[-1]
    at = 0
    for count in groups:
        left = jnp.concatenate([ref[...] for ref in refs[:8]], 0)
        right = jnp.concatenate([ref[...] for ref in refs[8 : 8 + count]], 0)
        refs = refs[8 + count :]
        width = right.shape[1]
        out_ref[:, at : at + width] = mul(left, right, TN).astype(bf16)
        at += width
    if copied:
        out_ref[:, at:] = refs[0][...]


def weight_grads(name, pieces, first, count, copied=None, held=None):
    width = sum(right[0].shape[1] for _, right in pieces)
    specs, args = [], []
    for left, right in pieces:
        specs += [pl.BlockSpec((ROWS, 256), lambda i: (0, i + first))] * 8
        specs += [pl.BlockSpec(r.shape, lambda i: (0, 0)) for r in right]
        args += list(left) + list(right)
    flops = 2 * 256 * count * 8 * ROWS * width
    if copied is not None:
        specs.append(pl.BlockSpec((256, copied.shape[1]), lambda i: (i + first, 0)))
        args.append(copied)
        width += copied.shape[1]
    aliases = {}
    if held is not None:
        aliases = {len(args): 0}
        specs.append(pl.BlockSpec(memory_space=pl.ANY))
        args.append(held)
    return call(
        functools.partial(outer_sums, [len(right) for _, right in pieces], copied is not None),
        name,
        jax.ShapeDtypeStruct((D, width), bf16),
        flops,
        limit=24,
        grid=(count,),
        in_specs=specs,
        out_specs=pl.BlockSpec((256, width), lambda i: (i + first, 0)),
        input_output_aliases=aliases,
    )(*args)


def flat(pairs):
    return [block for pair in pairs for block in pair]


def per_device(
    layer_in,
    cotangent,
    lengths,
    weights,
    weights_first,
    weights_second,
    gains,
    gains_first,
    gains_second,
):
    zh, y, zl, x, core = (lax.axis_index(name) for name in EVERY)
    slot = (zl * 4 + x) * 2 + zh
    length = lax.dynamic_index_in_dim(lengths, slot, 0, keepdims=False)

    def shape(*dims, kind=bf16):
        return jax.ShapeDtypeStruct(dims, kind)

    row_gains = gains.astype(bf16).astype(f32).T
    attn_cols, mlp_cols = call(
        prepare,
        "prepare",
        [shape(T, 16, N_ATTN + DOWN), shape(T, 16, GU)],
        10**8,
        limit=24,
        in_specs=whole(2),
        out_specs=whole(2),
    )(row_gains, weights)

    starts = []
    for k in range(4):
        zero, one = (y ^ k) * ROWS, ((y ^ k) + 4) * ROWS
        starts += [jnp.where(core == 0, zero, one), jnp.where(core == 0, one, zero)]
    starts.append(length)
    starts += [((zh * 2 + zl) ^ k) * 512 for k in range(4)]
    starts += [(x ^ k) * ROWS for k in range(4)]
    starts.append(jnp.where(zh == core, 1, 0))
    info = jnp.stack(starts).astype(jnp.int32)

    row_block = shape(ROWS, D)
    smem = [pl.BlockSpec(memory_space=pltpu.SMEM)]

    y_axis, z_axis = "y", ("zh", "zl")
    z = zh * 2 + zl

    def small(body, name, outs, *args, scalars=False):
        return call(
            body,
            name,
            outs,
            10**6,
            in_specs=(smem if scalars else []) + whole(len(args)),
            out_specs=whole(len(outs)),
        )(*((info,) if scalars else ()), *args)

    half_block = shape(ROWS // 2, D)

    def cut_halves(near):
        rows, width = near[0].shape
        return small(cut, "halves", [shape(rows // 2, width)] * 2, *near)

    def far_sums(kept, came):
        return small(far_sum, "far_sum", [half_block] * 2, kept, came)

    def join(one, three, came):
        outs = [shape(*one[0].shape)] * 2
        return small(near_join, "near_join", outs, *one, *three, *came)

    other = other_half(jnp.concatenate([layer_in, cotangent], 0))
    matrix = order_matrix()
    other, wide_rows, matrix, info = tie(other, exchange(attn_cols), matrix, info)
    wide_all = lax.all_gather(wide_rows, PLANE, axis=0, tiled=True)
    inputs, own = small(
        take_inputs, "take_inputs", [row_block] * 2, layer_in[0], other, matrix, scalars=True
    )

    near = send_near(own, y_axis)
    near, halves = tie(near, cut_halves(near))
    far = send_far(halves, y_axis)
    swaps = [swap_core(block) for block in (own, *near)]
    (cot,) = small(
        take_cotangent, "take_cotangent", [row_block], cotangent[0], other, matrix, scalars=True
    )
    table = rope_tables(jnp.arange(T * ROWS, dtype=jnp.int32))
    far, swaps, cot, table, mlp_cols = tie(far, swaps, cot, table, mlp_cols)
    mlp_both = exchange_cores(mlp_cols)
    cot_near = send_near(cot, y_axis)
    far = jnp.concatenate(far, 0)
    swaps.append(swap_core(far))
    cot_near, swaps, cot_swap, mlp_both = tie(cot_near, swaps, swap_core(cot), mlp_both)
    cot_near, halves = tie(cot_near, cut_halves(cot_near))
    cot_far = send_far(halves, y_axis)
    near_swaps = [swap_core(block) for block in cot_near]
    cot_far, near_swaps, mlp_rows, swaps = tie(
        cot_far, near_swaps, arrange(exchange_y(mlp_both)), swaps
    )
    gate_all = lax.all_gather(mlp_rows, PLANE, axis=0, tiled=True)
    cot_far = jnp.concatenate(cot_far, 0)
    mlp_grad = [
        (cot, cot_swap),
        (cot_near[0], near_swaps[0]),
        (cot_far, swap_core(cot_far)),
        (cot_near[1], near_swaps[1]),
    ]
    normed = list(zip((own, near[0], far, near[1]), (swaps[0], swaps[1], swaps[3], swaps[2])))

    def run_project(*args):
        return call(
            project,
            "project",
            [
                shape(4, GROUP_HEADS * QB, HD),
                shape(4, QB, HD),
                shape(4, QB, HD),
                shape(4, HD, QB),
                shape(4, HD, QB),
                shape(D, N_QKV),
                shape(D, Q_LOC),
            ],
            2 * 10**9,
            limit=58,
            scratch=[
                pltpu.VMEM((T * ROWS, N_QKV), f32),
                pltpu.VMEM((T * ROWS, D), bf16),
                pltpu.SemaphoreType.DMA((8,)),
                pltpu.SemaphoreType.DMA((2,)),
            ],
            in_specs=smem + anywhere(9) + whole(1),
            out_specs=whole(7),
        )(info, *args)

    def run_attend(*args):
        return call(
            attend,
            "attend",
            [shape(T * ROWS, Q_LOC), shape(4, 1, GROUP_HEADS * QB, kind=f32)],
            4 * 10**9,
            scratch=[pltpu.VMEM((T * ROWS, Q_LOC), bf16)],
            in_specs=smem + whole(3),
            out_specs=whole(2),
        )(info, *args)

    def run_terms(name, steps, rows, weight):
        outs = call(
            functools.partial(row_terms, steps),
            name,
            [row_block] * (2 * len(steps)),
            10**9 * len(steps),
            in_specs=whole(2),
            out_specs=whole(2 * len(steps)),
        )(rows, weight)
        return {k: outs[2 * i : 2 * i + 2] for i, k in enumerate(steps)}

    def run_mlp(*args):
        return call(
            mlp_pair,
            "mlp_pair",
            [shape(2 * ROWS, DOWN), shape(2 * ROWS, GU)] + [row_block] * 4,
            6 * 10**9,
            scratch=[
                pltpu.VMEM((2 * ROWS, DOWN), f32),
                pltpu.VMEM((2 * ROWS, D), bf16),
                pltpu.VMEM((2 * ROWS, D), bf16),
                pltpu.SemaphoreType.DMA((2,)),
                pltpu.SemaphoreType.DMA((2,)),
            ],
            in_specs=anywhere(4) + whole(2),
            out_specs=whole(6),
        )(*args, gate_all, wide_all)

    def run_head_grads(*args):
        return call(
            head_grads,
            "head_grads",
            shape(2 * ROWS, Q_LOC),
            10**9,
            scratch=[pltpu.VMEM((2 * ROWS, D), bf16), pltpu.SemaphoreType.DMA((2,))],
            in_specs=anywhere(2) + whole(1),
            out_specs=pl.BlockSpec(memory_space=pltpu.VMEM),
        )(*args, w_all)

    def run_backward(first, count, args, blocks=()):
        state = [
            shape(4, QB, HD, kind=f32),
            shape(4, QB, HD, kind=f32),
            shape(T * ROWS, Q_LOC, kind=f32),
        ]
        rows = pltpu.VMEM((T * ROWS, Q_LOC), f32)
        scratch = [rows, rows]
        last = first + count == 4
        if last:
            scratch += [pltpu.VMEM(v.shape, f32) for v in state]
            scratch += [pltpu.VMEM((T * ROWS, D), bf16), pltpu.SemaphoreType.DMA((8,))]
        return call(
            functools.partial(attention_backward, first, count),
            "attention_backward",
            [shape(T * ROWS, N_QKV), shape(D, Q_LOC)] if last else state,
            4 * 10**9 * count,
            scratch=scratch,
            in_specs=smem + whole(len(args)) + hbm(len(blocks)),
            out_specs=whole(2 if last else 3),
        )(info, *args, *blocks)

    def near_y(own):
        return send_near(own, y_axis)

    def far_y(halves):
        return send_far(halves, y_axis)

    def sum_far_y(halves):
        return sum_far(halves, y_axis)

    def sum_near_y(joined):
        return sum_near(joined, y_axis)

    def with_other(pair):
        return pair[0], swap_core(pair[1])

    query, key, value, key_t, value_t, q_all, w_all = run_project(*flat(normed), wide_all, table)
    attended, logs = run_attend(query, key, value_t)
    terms = run_terms("branch_terms", (2,), attended, w_all)
    sent = swap_core(terms[2][1])
    terms.update(run_terms("branch_terms", (1, 3, 0), attended, w_all))
    halves = far_sums(terms[2][0], sent)
    came, one, three = lax.optimization_barrier(
        (sum_far_y(halves), with_other(terms[1]), with_other(terms[3]))
    )
    joined = join(one, three, came)
    came, own = lax.optimization_barrier((sum_near_y(joined), with_other(terms[0])))
    middle, own = small(
        take_middle,
        "take_middle",
        [shape(ROWS, D, kind=f32), row_block],
        *own,
        *came,
        inputs,
    )

    normed_mid = {0: (own, swap_core(own))}
    mlp = {}
    near, mlp[0] = during(near_y, own, run_mlp, *normed_mid[0], *mlp_grad[0])
    halves = cut_halves(near)
    normed_mid[3] = (near[1], swap_core(near[1]))
    normed_mid[1] = (near[0], swap_core(near[0]))
    far, mlp[3] = during(far_y, halves, run_mlp, *normed_mid[3], *mlp_grad[3])
    far = jnp.concatenate(far, 0)
    normed_mid[2] = (far, swap_core(far))
    mlp[2] = run_mlp(*normed_mid[2], *mlp_grad[2])
    halves = far_sums(*with_other(mlp[2][2:4]))
    came, mlp[1] = during(sum_far_y, halves, run_mlp, *normed_mid[1], *mlp_grad[1])
    order_of = (0, 3, 2, 1)
    pieces = [
        (flat([normed_mid[k] for k in order_of]), [mlp[k][1] for k in order_of]),
        (flat([mlp_grad[k] for k in order_of]), [mlp[k][0] for k in order_of]),
    ]

    joined = join(with_other(mlp[1][2:4]), with_other(mlp[3][2:4]), came)
    came, (mlp_part, kept) = during(
        sum_near_y,
        joined,
        lambda pieces, pair: (
            weight_grads("mlp_weight_grads", pieces, 0, 8),
            with_other(pair),
        ),
        pieces,
        mlp[0][2:4],
    )
    mlp_sum = lax.psum_scatter(mlp_part, PLANE, scatter_dimension=0, tiled=True)
    middle_grad, own = small(
        middle_grads,
        "middle_grads",
        [shape(ROWS, D, kind=f32), row_block],
        *kept,
        *came,
        middle,
        cot,
    )

    own_swap, *sent = tie(swap_core(own), *[mlp[k][5] for k in range(4)])
    near = near_y(own)
    near, *sent = tie(near, *[swap_core(part) for part in sent])
    pair = own, own_swap
    outs = [(mlp[k][4], sent[k]) for k in range(4)]
    branch_grad = {0: pair}
    heads = {}
    halves = cut_halves(near)
    for k in (1, 3):
        branch_grad[k] = (near[k // 2], swap_core(near[k // 2]))

    far, (heads[0], heads[1], heads[3]) = during(
        far_y,
        halves,
        lambda *pairs: tuple(run_head_grads(*pair) for pair in pairs),
        *[branch_grad[k] for k in (0, 1, 3)],
    )
    far = jnp.concatenate(far, 0)
    branch_grad[2] = (far, swap_core(far))
    heads[2] = run_head_grads(*branch_grad[2])

    common = (*[heads[k] for k in range(4)], attended, table, query, key, value, key_t, logs)
    came, state = during(sum_far_y, far_sums(*outs[2]), lambda *a: run_backward(0, 3, a), *common)
    joined = join(outs[1], outs[3], came)

    came, (proj_grad, out_part) = during(
        sum_near_y,
        joined,
        lambda *a: run_backward(3, 1, a, flat([branch_grad[k] for k in range(4)])),
        *common,
        *state,
    )
    terms = run_terms("input_terms", (2,), proj_grad, q_all)
    sent = swap_core(terms[2][1])
    halves = far_sums(terms[2][0], sent)
    steps = (1, 3, 0)

    def run_last(rows, normed, held):
        wide = N_QKV + Q_LOC
        outs = call(
            functools.partial(last_grads, steps),
            "last_grads",
            [row_block] * 6 + [shape(256, wide)] * 2 + [shape(512, wide)] * 3,
            10**9,
            limit=58,
            scratch=[
                pltpu.VMEM((T * ROWS, D), bf16),
                pltpu.VMEM((D, N_QKV), bf16),
                pltpu.SemaphoreType.DMA((8,)),
                pltpu.SemaphoreType.DMA((16,)),
            ],
            in_specs=smem + whole(2) + anywhere(9),
            out_specs=whole(11),
        )(info, rows, q_all, *normed, held)
        return {k: outs[2 * i : 2 * i + 2] for i, k in enumerate(steps)}, outs[6:]

    layer_low, streams = small(
        give_output,
        "give_output",
        [row_block, shape(8, 128, kind=f32)],
        *outs[0],
        *came,
        middle,
        inputs,
        matrix,
        scalars=True,
    )
    proj_grad, streams, layer_low = tie(proj_grad, streams, layer_low)
    came_far, came_streams, other_out, (rest, by_x) = tie(
        sum_far_y(halves),
        trade(streams, "x", 1),
        other_half(layer_low),
        run_last(proj_grad, flat(normed), out_part),
    )
    streams = streams + came_streams
    far_a, far_b, one_x, three_x, own_x = by_x
    line = sum_far((far_a, far_b), "x")
    joined = join(with_other(rest[1]), with_other(rest[3]), came_far)
    streams = streams + trade(streams, "x", 2)
    line = sum_near(join((one_x,), (three_x,), line), "x")
    kept = rest[0]
    came_near = sum_near_y(joined)
    mlp_both = exchange_cores(mlp_sum)
    line, came_near, mlp_both = tie(line, came_near, mlp_both)
    layer_out = jnp.where(zh == core, layer_low, other_out)
    z_blocks = small(
        sum_lines,
        "sum_lines",
        [shape(ROWS, N_QKV + Q_LOC, kind=f32)] + [shape(ROWS, N_QKV + Q_LOC + 128)] * 3,
        own_x,
        *line,
        streams,
        scalars=True,
    )
    own_z, mlp_both = tie(z_blocks[0], mlp_both)
    z_blocks = [own_z, *z_blocks[1:]]
    line = [trade(z_blocks[k], z_axis, k) for k in (1, 2, 3)]
    kept = with_other(kept)
    mlp_sum = exchange_y(mlp_both)
    (input_low,) = small(
        give_input_grad,
        "give_input_grad",
        [row_block],
        *kept,
        *came_near,
        inputs,
        middle_grad,
        matrix,
    )
    weight_args = (weights, weights_first, weights_second)
    columns = [shape(16, weights.shape[1], kind=f32)] * 3

    def buffers(width, count):
        return [pltpu.VMEM((16, width), f32)] * count + [pltpu.SemaphoreType.DMA((3,))]

    def run_update_mlp(mlp_sum):
        return call(
            update_mlp,
            "update_mlp",
            columns + [shape(16, 128, kind=f32)],
            10**8,
            scratch=buffers(weights.shape[1] - ATTN_COLS, 3),
            in_specs=whole(5),
            out_specs=anywhere(3) + whole(1),
        )(row_gains, mlp_sum, *weight_args)

    line, input_low, mlp_sum = tie(line, input_low, mlp_sum)
    (attn_parts,) = small(
        plane_parts,
        "plane_parts",
        [shape(T, 16, N_QKV + Q_LOC + 256)],
        z_blocks[0],
        *line,
        streams,
    )
    input_out = swap_halves(input_low).astype(f32)
    attn_both, mlp_sum = tie(exchange_cores(attn_parts), mlp_sum)
    attn_parts, (*held, second_sums) = tie(
        exchange_y(attn_both), run_update_mlp(arrange(mlp_sum).reshape(T, 16, -1))
    )
    attn_parts = arrange(attn_parts).reshape(T, 16, -1)
    weights_new, weights_first_new, weights_second_new, first_sums, streams = call(
        update_attention,
        "update_attention",
        columns + [shape(16, 128, kind=f32), shape(8, 128, kind=f32)],
        10**7,
        scratch=buffers(ATTN_COLS, 6),
        in_specs=whole(2) + anywhere(6),
        out_specs=anywhere(3) + whole(2),
        input_output_aliases={5: 0, 6: 1, 7: 2},
    )(row_gains, attn_parts, *weight_args, *held)
    gain_grad = jnp.stack([first_sums[:, 0], second_sums[:, 0]])
    stream_sums = jnp.sum(streams[:5], 1)
    valid_count = jnp.sum(lengths).astype(f32) * D
    stream_rms = jnp.sqrt(stream_sums / valid_count)

    gains_new, gains_first_new, gains_second_new = adam(
        gains, gains_first, gains_second, gain_grad, rate_gains, 0.0
    )
    return (
        layer_out[None],
        input_out[None],
        weights_new,
        weights_first_new,
        weights_second_new,
        gains_new,
        gains_first_new,
        gains_second_new,
        stream_rms,
    )


def solution(mesh):
    fine = Mesh(mesh.devices.reshape(2, 4, 2, 4, 2), EVERY)
    ctx = ("zh", "y")
    head = ("zl", "x", "core")
    tokens = P(head, ctx, None)
    matrices = P(EVERY, None)
    vectors = P(None, EVERY)
    return jax.shard_map(
        per_device,
        mesh=fine,
        in_specs=(tokens, tokens, P()) + (matrices,) * 3 + (vectors,) * 3,
        out_specs=(tokens, tokens) + (matrices,) * 3 + (vectors,) * 3 + (P(),),
        check_vma=False,
    )
```
